32 devices in a mesh: phase: 4 (over x, core), seq: 8 (over z, y).
Axes of the slice: x: 2, y: 2, z: 4, core: 2. Of those that a mesh axis runs over, the one named last changes fastest.
Arguments:
- frames: bfloat16 [4, 1280, 1024], P('phase', 'seq'), may hold values from -6 to 6
- lengths: int32 [4, 8], P('phase'), may hold values from 1 to 640, 1280 in all within a row
- w_query: bfloat16 [4, 1024, 1024], P('phase', None, 'seq'), may hold values from -1 to 1
- w_key: bfloat16 [4, 1024, 1024], P('phase', None, 'seq'), may hold values from -1 to 1
- w_value: bfloat16 [4, 1024, 1024], P('phase', None, 'seq'), may hold values from -0.1875 to 0.1875
- w_output: bfloat16 [4, 1024, 1024], P('phase', None, 'seq'), may hold values from -0.1875 to 0.1875
- conv_in: bfloat16 [4, 1024, 2048], P('phase', None, 'seq'), may hold values from -0.1875 to 0.1875
- conv_taps: bfloat16 [4, 31, 1024], P('phase'), may hold values from -1 to 1
- conv_out: bfloat16 [4, 1024, 1024], P('phase', None, 'seq'), may hold values from -0.1875 to 0.1875
Outputs:
- handed: bfloat16 [4, 1280, 1024], P('phase', 'seq')
The draws below stay inside these ranges and needn't reach their ends.
Inputs may be any that keep to these rules, and one draw needn't show every extreme that they name: Each phase's lengths sum to 1280 and the largest equals 640.
All inputs are finite; a program needn't handle non-finite values.
Results may differ from the reference program's by a relative error of at most 0.0085.
Values may be sent and summed in bfloat16 or wider, within the bound.
A program may use at most 64 MiB of HBM per device.

```python
import math
import jax
import jax.numpy as jnp
import numpy as np
from jax import lax

D = 1024
HEADS = 16
KERNEL = 31
UTTS = 8
FRAMES = 1280
N_PHASE = 4


def projection(key, salt):
    shared = jax.random.normal(jax.random.fold_in(key, 101), (N_PHASE, D, D), jnp.float32)
    own = jax.random.normal(jax.random.fold_in(key, salt), (N_PHASE, D, D), jnp.float32)
    mixed = 0.6 * shared + 0.8 * own
    return jnp.clip(mixed / math.sqrt(D), -1.0, 1.0).astype(jnp.bfloat16)


def draw_w_query(key, part):
    return projection(key, 102)


def draw_w_key(key, part):
    return projection(key, 103)


def steps_of(stream_key, dims, shards, least, top_value):
    def one(dim, blocks):
        steps = jax.random.uniform(jax.random.fold_in(jax.random.fold_in(stream_key, 6), dim), (blocks,), jnp.float32, least / len(shards), top_value / len(shards))
        return jnp.repeat(jnp.exp(steps), dims[dim] // blocks).reshape((-1,) + (1,) * (len(dims) - dim - 1))

    loudness = one(*shards[0])
    for cut in shards[1:]:
        loudness = loudness * one(*cut)
    return loudness


def length_profile(amount, total, most, slope):
    loads = [(1 << 20) // math.isqrt(grade ** slope) + 1 for grade in range(2, amount + 1)]
    rest, holding = total - most - (amount - 1), [1] * (amount - 1)
    while rest > 0:
        candidates = [i for i in range(amount - 1) if holding[i] < most]
        mass, left = sum([loads[i] for i in candidates]), rest
        for i in candidates:
            more = min(most - holding[i], max(1, left * loads[i] // mass), rest)
            holding[i] = holding[i] + more
            rest = rest - more
    return np.array([most] + holding)


def uneven_parts(key, number_of, total, limit, skew):
    if number_of == 2:
        one = jax.random.randint(key, (), max(1, total - limit), min(limit, total - 1) + 1)
        return jnp.stack([one, total - one])
    sizes = jnp.asarray(length_profile(number_of, total, limit, skew), jnp.int32)
    twos = (number_of - 1) // 2
    giver, sink = sizes[1:1 + 2 * twos:2], sizes[2:2 + 2 * twos:2]
    slack = jnp.minimum(giver - 1, limit - sink)
    moved = jax.random.randint(jax.random.fold_in(key, 1), (twos,), 0, 1 << 20) % (slack + 1)
    sizes = sizes.at[1:1 + 2 * twos:2].set(giver - moved).at[2:2 + 2 * twos:2].set(sink + moved)
    return sizes[jax.random.permutation(jax.random.fold_in(key, 2), number_of)]


def scatter_about(stream_key, extent, deviation, most, split=(), held_as=jnp.bfloat16):
    gain = steps_of(stream_key, extent, split, -0.22, 0.18) if split else 1.0
    values = jax.random.normal(stream_key, extent, jnp.float32) * deviation * gain
    return jnp.minimum(jnp.maximum(values, -most), most).astype(held_as)


def setup_inputs(seed: int = 0) -> dict:
    keys = jax.random.split(jax.random.key(seed), 10)
    return {
        "frames": scatter_about(keys[0], (N_PHASE, FRAMES, D), 1.0, 6.0, ((0, 4), (1, 8))),
        "lengths": jax.vmap(lambda own: uneven_parts(own, UTTS, FRAMES, FRAMES // 2, 2))(jax.random.split(keys[1], N_PHASE)).reshape((N_PHASE, UTTS)).astype(jnp.int32),
        "w_query": draw_w_query(jax.random.fold_in(keys[9], 71), 0),
        "w_key": draw_w_key(jax.random.fold_in(keys[9], 71), 0),
        "w_value": scatter_about(keys[4], (N_PHASE, D, D), D ** -0.5, 0.1875, ((0, 4), (2, 8))),
        "w_output": scatter_about(keys[5], (N_PHASE, D, D), D ** -0.5, 0.1875, ((0, 4), (2, 8))),
        "conv_in": scatter_about(keys[6], (N_PHASE, D, 2 * D), D ** -0.5, 0.1875, ((0, 4), (2, 8))),
        "conv_taps": scatter_about(keys[7], (N_PHASE, KERNEL, D), KERNEL ** -0.5, 1.0, ((0, 4),)),
        "conv_out": scatter_about(keys[8], (N_PHASE, D, D), D ** -0.5, 0.1875, ((0, 4), (2, 8))),
    }


def layer_norm(values):
    centre = values - lax.optimization_barrier(jnp.mean(values, axis=-1, keepdims=True))
    spread = lax.optimization_barrier(jnp.mean(centre * centre, axis=-1, keepdims=True))
    return centre * lax.rsqrt(spread + 1e-05)

def segment_ids(positions, lengths):
    bounds = jnp.cumsum(lengths).astype(jnp.int32)
    return lax.optimization_barrier(jnp.sum((positions[:, None] >= bounds[None, :]).astype(jnp.int32), axis=1)).astype(jnp.int32)

def conformer_block(hidden, lengths, w_query, w_key, w_value, w_output, conv_in, conv_taps, conv_out):
    total_rows = hidden.shape[0]
    width = hidden.shape[1]
    head_size = width // HEADS
    scale = 1.0 / math.sqrt(head_size)
    normed = layer_norm(hidden.astype(jnp.float32)).astype(jnp.bfloat16)
    query = jnp.dot(normed, w_query, preferred_element_type=jnp.float32).astype(jnp.bfloat16)
    key_proj = jnp.dot(normed, w_key, preferred_element_type=jnp.float32).astype(jnp.bfloat16)
    value_proj = jnp.dot(normed, w_value, preferred_element_type=jnp.float32).astype(jnp.bfloat16)
    segment = segment_ids(jnp.arange(total_rows, dtype=jnp.int32), lengths)
    same_utt = segment[:, None] == segment[None, :]

    def one_head(operands):
        head_query, head_key, head_value = operands
        scores = jnp.dot(head_query, head_key.T, preferred_element_type=jnp.float32) * scale
        scores = jnp.where(same_utt, scores, -1e+30)
        peak = lax.optimization_barrier(jnp.max(scores, axis=1, keepdims=True))
        expw = jnp.where(same_utt, jnp.exp(scores - peak), 0.0)
        total_weight = lax.optimization_barrier(jnp.sum(expw, axis=1, keepdims=True))
        mixed = jnp.dot(expw.astype(jnp.bfloat16), head_value, preferred_element_type=jnp.float32) / total_weight
        return mixed.astype(jnp.bfloat16)

    def split_heads(matrix):
        return matrix.reshape(total_rows, HEADS, head_size).transpose(1, 0, 2)
    attended = lax.map(one_head, (split_heads(query), split_heads(key_proj), split_heads(value_proj)))
    attended = attended.transpose(1, 0, 2).reshape(total_rows, width)
    after_attn = hidden.astype(jnp.float32) + jnp.dot(attended, w_output, preferred_element_type=jnp.float32)
    conv_normed = layer_norm(after_attn).astype(jnp.bfloat16)
    gates = jnp.dot(conv_normed, conv_in, preferred_element_type=jnp.float32)
    glu = (gates[:, :width] * jax.nn.sigmoid(gates[:, width:])).astype(jnp.bfloat16)
    reach = KERNEL // 2
    padded = jnp.pad(glu, ((reach, reach), (0, 0)))
    padded_seg = jnp.pad(segment, (reach, reach), constant_values=-1)
    depthwise = jnp.zeros((total_rows, width), jnp.float32)
    for offset in range(KERNEL):
        keep = padded_seg[offset:offset + total_rows] == segment
        term = padded[offset:offset + total_rows].astype(jnp.float32) * conv_taps[offset].astype(jnp.float32)
        depthwise = depthwise + jnp.where(keep[:, None], term, 0.0)
    conv_act = layer_norm(depthwise)
    conv_act = (conv_act * jax.nn.sigmoid(conv_act)).astype(jnp.bfloat16)
    result = after_attn + jnp.dot(conv_act, conv_out, preferred_element_type=jnp.float32)
    return result.astype(jnp.bfloat16)

def reference(frames, lengths, w_query, w_key, w_value, w_output, conv_in, conv_taps, conv_out):
    outputs = []
    for phase_idx in range(N_PHASE):
        outputs.append(conformer_block(frames[phase_idx], lengths[phase_idx], w_query[phase_idx], w_key[phase_idx], w_value[phase_idx], w_output[phase_idx], conv_in[phase_idx], conv_taps[phase_idx], conv_out[phase_idx]))
    stacked = jnp.stack(outputs)
    return jnp.roll(stacked, 1, axis=0)
```

```python
import math

import jax
import jax.numpy as jnp
from jax import lax
from jax.sharding import PartitionSpec as P

HEADS = 16
KERNEL = 31


def padded_2(block, sides, width):
    for axis, dim in sides:
        count = lax.axis_size(axis)
        forward = [(i, i + 1) for i in range(count - 1)]
        backward = [(target, source) for source, target in forward]
        low = lax.ppermute(
            lax.slice_in_dim(block, block.shape[dim] - width, None, axis=dim), axis, forward
        )
        high = lax.ppermute(lax.slice_in_dim(block, 0, width, axis=dim), axis, backward)
        block = jnp.concatenate([low, block, high], axis=dim)
    return block


def passed_along(block, axis, distance):
    devices = range(lax.axis_size(axis))
    route = [((i - distance) % len(devices), i) for i in devices]
    return lax.ppermute(block, axis, route)


def layer_norm(values):
    centre = values - jnp.mean(values, axis=-1, keepdims=True)
    spread = jnp.mean(centre * centre, axis=-1, keepdims=True)
    return centre * lax.rsqrt(spread + 1e-05)


def segment_ids(positions, lengths):
    order = jnp.arange(lengths.shape[0], dtype=jnp.int32)
    bounds = jnp.sum(jnp.where(order[None, :] <= order[:, None], lengths[None, :], 0), axis=1)
    return jnp.sum((positions[:, None] >= bounds[None, :]).astype(jnp.int32), axis=1)


def body(frames, lengths, w_query, w_key, w_value, w_output, conv_in, conv_taps, conv_out):
    hidden = frames[0]
    utt_lengths = lengths[0]
    shards = lax.axis_size("seq")
    my_index = lax.axis_index("seq")
    local_rows = hidden.shape[0]
    width = hidden.shape[1]
    total_rows = local_rows * shards
    head_size = width // HEADS
    scale = 1.0 / math.sqrt(head_size)
    groups = min(HEADS, shards)
    group_heads = HEADS // groups
    parts = shards // groups
    part_rows = local_rows // parts
    group_width = group_heads * head_size
    full_query, full_key, full_value, full_output, full_conv_in, full_conv_out = (
        lax.all_gather(w_query[0], "seq", axis=1, tiled=True),
        lax.all_gather(w_key[0], "seq", axis=1, tiled=True),
        lax.all_gather(w_value[0], "seq", axis=1, tiled=True),
        lax.all_gather(w_output[0], "seq", axis=1, tiled=True),
        lax.all_gather(conv_in[0], "seq", axis=1, tiled=True),
        lax.all_gather(conv_out[0], "seq", axis=1, tiled=True),
    )
    normed = layer_norm(hidden.astype(jnp.float32)).astype(jnp.bfloat16)
    query = jnp.dot(normed, full_query, preferred_element_type=jnp.float32).astype(jnp.bfloat16)
    key_proj = jnp.dot(normed, full_key, preferred_element_type=jnp.float32).astype(jnp.bfloat16)
    value_proj = jnp.dot(normed, full_value, preferred_element_type=jnp.float32).astype(
        jnp.bfloat16
    )
    shaped = query.reshape(parts, part_rows, groups, group_width).transpose(2, 0, 1, 3)
    query_pieces = shaped.reshape(shards, part_rows, group_width)
    kv_local = jnp.concatenate(
        [
            key_proj.reshape(local_rows, groups, group_width),
            value_proj.reshape(local_rows, groups, group_width),
        ],
        axis=2,
    )
    copies = jnp.broadcast_to(
        kv_local.transpose(1, 0, 2)[:, None], (groups, parts, local_rows, 2 * group_width)
    )
    copies = copies.reshape(shards, local_rows, 2 * group_width)
    query_got, kv_got = (
        lax.all_to_all(query_pieces, "seq", split_axis=0, concat_axis=0, tiled=True),
        lax.all_to_all(copies, "seq", split_axis=0, concat_axis=0, tiled=True),
    )
    key_value = kv_got.reshape(total_rows, 2 * group_width)
    count = shards * part_rows
    my_part = my_index % parts
    row_ids = jnp.arange(count, dtype=jnp.int32)
    query_pos = row_ids // part_rows * local_rows + my_part * part_rows + row_ids % part_rows
    queries = query_got.reshape(count, group_heads, head_size)
    key_rows = key_value[:, :group_width].reshape(total_rows, group_heads, head_size)
    value_rows = key_value[:, group_width:].reshape(total_rows, group_heads, head_size)
    seg_all = segment_ids(jnp.arange(total_rows, dtype=jnp.int32), utt_lengths)
    seg_query = segment_ids(query_pos, utt_lengths)
    query_block = math.gcd(512, count)
    blocks = count // query_block

    def attend_block(operands):
        block_query, block_seg = operands
        scores = (
            jnp.einsum("qhd,khd->hqk", block_query, key_rows, preferred_element_type=jnp.float32)
            * scale
        )
        allowed = (block_seg[:, None] == seg_all[None, :])[None]
        scores = jnp.where(allowed, scores, -1e30)
        peak = jnp.max(scores, axis=2, keepdims=True)
        expw = jnp.where(allowed, jnp.exp(scores - peak), 0.0)
        total_weight = jnp.sum(expw, axis=2)
        mixed = jnp.einsum(
            "hqk,khd->hqd",
            expw.astype(jnp.bfloat16),
            value_rows,
            preferred_element_type=jnp.float32,
        )
        mixed = mixed / total_weight[:, :, None]
        return mixed.transpose(1, 0, 2).astype(jnp.bfloat16)

    attended = lax.map(
        attend_block,
        (
            queries.reshape(blocks, query_block, group_heads, head_size),
            seg_query.reshape(blocks, query_block),
        ),
    )
    outgoing = attended.reshape(shards, part_rows, group_width)
    returned = lax.all_to_all(outgoing, "seq", split_axis=0, concat_axis=0, tiled=True)
    attended_local = (
        returned.reshape(groups, parts, part_rows, group_width)
        .transpose(1, 2, 0, 3)
        .reshape(local_rows, width)
    )
    after_attn = hidden.astype(jnp.float32) + jnp.dot(
        attended_local, full_output, preferred_element_type=jnp.float32
    )
    conv_normed = layer_norm(after_attn).astype(jnp.bfloat16)
    gates = jnp.dot(conv_normed, full_conv_in, preferred_element_type=jnp.float32)
    glu = (gates[:, :width] * jax.nn.sigmoid(gates[:, width:])).astype(jnp.bfloat16)
    reach = KERNEL // 2
    padded = padded_2(glu, (("seq", 0),), KERNEL // 2)
    padded_pos = my_index * local_rows - reach + jnp.arange(local_rows + 2 * reach, dtype=jnp.int32)
    inside = (padded_pos >= 0) & (padded_pos < total_rows)
    padded_seg = jnp.where(inside, segment_ids(padded_pos, utt_lengths), -1)
    own_seg = padded_seg[reach : reach + local_rows]
    taps = conv_taps[0]
    depthwise = jnp.zeros((local_rows, width), jnp.float32)
    for offset in range(KERNEL):
        keep = padded_seg[offset : offset + local_rows] == own_seg
        term = padded[offset : offset + local_rows].astype(jnp.float32) * taps[offset].astype(
            jnp.float32
        )
        depthwise = depthwise + jnp.where(keep[:, None], term, 0.0)
    conv_act = layer_norm(depthwise)
    conv_act = (conv_act * jax.nn.sigmoid(conv_act)).astype(jnp.bfloat16)
    block_out = (
        after_attn + jnp.dot(conv_act, full_conv_out, preferred_element_type=jnp.float32)
    ).astype(jnp.bfloat16)
    passed = passed_along(block_out, "phase", 1)
    return passed[None]


def solution(mesh):
    in_specs = (
        P("phase", "seq", None),
        P("phase", None),
        P("phase", None, "seq"),
        P("phase", None, "seq"),
        P("phase", None, "seq"),
        P("phase", None, "seq"),
        P("phase", None, "seq"),
        P("phase", None, None),
        P("phase", None, "seq"),
    )
    out_specs = P("phase", "seq", None)
    return jax.shard_map(body, mesh=mesh, in_specs=in_specs, out_specs=out_specs, check_vma=False)
```

```python
import functools
import math

import jax
import jax.numpy as jnp
from jax import lax
from jax.experimental import pallas as pl
from jax.experimental.pallas import tpu as pltpu
from jax.sharding import PartitionSpec as P

HEADS = 16
KERNEL = 31
MESH = pl.DeviceIdType.MESH


def padded_2(block, sides, width):
    for axis, dim in sides:
        count = lax.axis_size(axis)
        forward = [(i, i + 1) for i in range(count - 1)]
        backward = [(target, source) for source, target in forward]
        low = lax.ppermute(
            lax.slice_in_dim(block, block.shape[dim] - width, None, axis=dim), axis, forward
        )
        high = lax.ppermute(lax.slice_in_dim(block, 0, width, axis=dim), axis, backward)
        block = jnp.concatenate([low, block, high], axis=dim)
    return block


def passed_along(block, axis, distance):
    devices = range(lax.axis_size(axis))
    route = [((i - distance) % len(devices), i) for i in devices]
    return lax.ppermute(block, axis, route)


def layer_norm(values):
    centre = values - jnp.mean(values, axis=-1, keepdims=True)
    spread = jnp.mean(centre * centre, axis=-1, keepdims=True)
    return centre * lax.rsqrt(spread + 1e-05)


def segment_ids(positions, lengths):
    order = jnp.arange(lengths.shape[0], dtype=jnp.int32)
    bounds = jnp.sum(jnp.where(order[None, :] <= order[:, None], lengths[None, :], 0), axis=1)
    return jnp.sum((positions[:, None] >= bounds[None, :]).astype(jnp.int32), axis=1)


def ring_index(place, shards):
    place = lax.rem(place + shards, shards)
    late = lax.div(place, shards // 2)
    return (1 - late) * (2 * place) + late * (2 * (shards - 1 - place) + 1)


def attention_kernel(
    shards,
    head_size,
    frames_ref,
    seg_row_ref,
    seg_col_ref,
    query_ref,
    key_ref,
    value_ref,
    w_a_ref,
    w_b_ref,
    w_c_ref,
    attended_ref,
    full_a_ref,
    full_b_ref,
    full_c_ref,
    normed,
    query,
    keys,
    values,
    outbox,
    send_sem,
    recv_sem,
    own_sem,
    out_send,
    out_recv,
):
    rows = frames_ref.shape[0]
    width = query_ref.shape[1]
    steps = shards // 2
    me = lax.axis_index("seq")
    odd = lax.rem(me, 2)
    place = (1 - odd) * lax.div(me, 2) + odd * (shards - 1 - lax.div(me, 2))
    right, left = ring_index(place + 1, shards), ring_index(place - 1, shards)

    barrier = pltpu.get_barrier_semaphore()
    for away in range(1, shards):
        peer = lax.rem(me + away, shards)
        pl.semaphore_signal(barrier, inc=1, device_id={"seq": peer}, device_id_type=MESH)

    own_rows = pl.ds(pl.multiple_of(me * rows, rows), rows)
    normed[own_rows, :] = layer_norm(frames_ref[...].astype(jnp.float32)).astype(jnp.bfloat16)
    pl.semaphore_wait(barrier, shards - 1)

    pairs = ((w_a_ref, full_a_ref), (w_b_ref, full_b_ref), (w_c_ref, full_c_ref))

    def view(load, owner, half):
        if load == 0:
            first, size = (0, rows) if half is None else (half * (rows // 2), rows // 2)
            return normed.at[pl.ds(pl.multiple_of(owner * rows + first, 16), size), :]
        own, full = pairs[load - 1]
        depth, part = own.shape
        first, size = (0, depth) if half is None else (half * (depth // 2), depth // 2)
        return full.at[pl.ds(first, size), pl.ds(pl.multiple_of(owner * part, 128), part)]

    def hop(load, step, way):
        half = way if step == steps - 1 else None
        owner = ring_index(place - step if way == 0 else place + step, shards)
        target = view(load, owner, half)
        source = target
        if load > 0 and step == 0:
            source = pairs[load - 1][0]
            if half is not None:
                depth = source.shape[0] // 2
                source = source.at[pl.ds(half * depth, depth), :]
        return pltpu.make_async_remote_copy(
            src_ref=source,
            dst_ref=target,
            send_sem=send_sem.at[load, step, way],
            recv_sem=recv_sem.at[load, step, way],
            device_id={"seq": right if way == 0 else left},
            device_id_type=MESH,
        )

    def arrive(load, step):
        for way in range(2):
            hop(load, step, way).wait_recv()

    def send(load, step):
        for way in range(2):
            hop(load, step, way).start()

    def project(owner):
        at = pl.ds(pl.multiple_of(owner * rows, rows), rows)
        block = normed[at, :]
        query[at, :] = (
            jnp.dot(block, query_ref[...], preferred_element_type=jnp.float32)
            .astype(jnp.bfloat16)
        ) * jnp.bfloat16(1.0 / math.sqrt(head_size))
        keys[at, :] = jnp.dot(
            block, key_ref[...], preferred_element_type=jnp.float32
        ).astype(jnp.bfloat16)
        values[at, :] = jnp.dot(
            block, value_ref[...], preferred_element_type=jnp.float32
        ).astype(jnp.bfloat16)

    kept = []
    send(0, 0)
    for load in (1, 2, 3):
        own, full = pairs[load - 1]
        part = own.shape[1]
        copy = pltpu.make_async_copy(
            own, full.at[:, pl.ds(pl.multiple_of(me * part, 128), part)], own_sem.at[load - 1]
        )
        copy.start()
        kept.append(copy)
    project(me)
    for step in range(steps):
        arrive(0, step)
        if step < steps - 1:
            send(0, step + 1)
        if step == steps - 2:
            for load in (1, 2, 3):
                send(load, 0)
        project(ring_index(place - 1 - step, shards))
        if step < steps - 1:
            project(ring_index(place + 1 + step, shards))

    lane = lax.broadcasted_iota(jnp.int32, (rows, width), 1)
    my_columns = pl.ds(pl.multiple_of(me * width, 128), width)

    def attend(owner):
        at = pl.ds(pl.multiple_of(owner * rows, rows), rows)
        block = query[at, :]
        allowed = seg_row_ref[at, :] == seg_col_ref[...]
        result = jnp.zeros((rows, width), jnp.float32)
        for head in range(width // head_size):
            mine = (lane >= head * head_size) & (lane < (head + 1) * head_size)
            scores = lax.dot_general(
                jnp.where(mine, block, jnp.bfloat16(0)),
                keys[...],
                (((1,), (1,)), ((), ())),
                preferred_element_type=jnp.float32,
            )
            scores = jnp.where(allowed, scores, -1e30)
            peak = jnp.max(scores, axis=1, keepdims=True)
            expw = jnp.exp(scores - peak)
            total = jnp.sum(expw, axis=1, keepdims=True)
            mixed = jnp.dot(
                expw.astype(jnp.bfloat16), values[...], preferred_element_type=jnp.float32
            )
            result = jnp.where(mine, mixed / total, result)
        return result.astype(jnp.bfloat16)

    def out_copy(away):
        peer = lax.rem(me + away, shards)
        return pltpu.make_async_remote_copy(
            src_ref=outbox.at[away - 1],
            dst_ref=attended_ref.at[:, my_columns],
            send_sem=out_send.at[away - 1],
            recv_sem=out_recv.at[away - 1],
            device_id={"seq": peer},
            device_id_type=MESH,
        )

    later = [(load, step) for step in range(steps) for load in (1, 2, 3)]
    moved = 0

    def forward(load, step):
        arrive(load, step)
        if step < steps - 1:
            send(load, step + 1)

    for away in range(1, shards + 1):
        if away < shards:
            outbox[away - 1] = attend(lax.rem(me + away, shards))
            out_copy(away).start()
        else:
            attended_ref[:, my_columns] = attend(me)
        if away * 4 % shards == 0 and away < shards:
            forward(*later[moved])
            moved += 1
    for load, step in later[moved:]:
        forward(load, step)
    for away in range(1, shards):
        out_copy(away).wait()
    for copy in kept:
        copy.wait()
    for load in range(4):
        for step in range(steps):
            for way in range(2):
                hop(load, step, way).wait_send()


def attention_call(shards, hidden, segments, w_query, w_key, w_value, rest):
    rows, depth = hidden.shape
    width = w_query.shape[1]
    total = rows * shards
    steps = shards // 2
    vmem = pl.BlockSpec(memory_space=pltpu.VMEM)
    anywhere = pl.BlockSpec(memory_space=pl.ANY)
    dma = pltpu.SemaphoreType.DMA
    return pl.pallas_call(
        functools.partial(attention_kernel, shards, depth // HEADS),
        out_shape=[jax.ShapeDtypeStruct((rows, shards * width), jnp.bfloat16)]
        + [jax.ShapeDtypeStruct((w.shape[0], w.shape[1] * shards), w.dtype) for w in rest],
        in_specs=[vmem] * 6 + [anywhere] * 3,
        out_specs=[vmem] + [anywhere] * 3,
        scratch_shapes=[
            pltpu.VMEM((total, depth), jnp.bfloat16),
            pltpu.VMEM((total, width), jnp.bfloat16),
            pltpu.VMEM((total, width), jnp.bfloat16),
            pltpu.VMEM((total, width), jnp.bfloat16),
            pltpu.VMEM((shards - 1, rows, width), jnp.bfloat16),
            dma((4, steps, 2)),
            dma((4, steps, 2)),
            dma((3,)),
            dma((shards - 1,)),
            dma((shards - 1,)),
        ],
        compiler_params=pltpu.CompilerParams(
            collective_id=0, has_side_effects=True, vmem_limit_bytes=48 * 1024 * 1024
        ),
        cost_estimate=pl.CostEstimate(
            flops=2 * total * width * (3 * depth + 4 * total),
            bytes_accessed=20_000_000,
            transcendentals=total * total * 2,
        ),
    )(hidden, segments[:, None], segments[None, :], w_query, w_key, w_value, *rest)


def attention_general(hidden, utt_lengths, w_query, w_key, w_value, w_output, conv_in, conv_out):
    shards = lax.axis_size("seq")
    my_index = lax.axis_index("seq")
    local_rows = hidden.shape[0]
    width = hidden.shape[1]
    total_rows = local_rows * shards
    head_size = width // HEADS
    scale = 1.0 / math.sqrt(head_size)
    groups = min(HEADS, shards)
    group_heads = HEADS // groups
    parts = shards // groups
    part_rows = local_rows // parts
    group_width = group_heads * head_size
    full_query, full_key, full_value, full_output, full_conv_in, full_conv_out = (
        lax.all_gather(w_query, "seq", axis=1, tiled=True),
        lax.all_gather(w_key, "seq", axis=1, tiled=True),
        lax.all_gather(w_value, "seq", axis=1, tiled=True),
        lax.all_gather(w_output, "seq", axis=1, tiled=True),
        lax.all_gather(conv_in, "seq", axis=1, tiled=True),
        lax.all_gather(conv_out, "seq", axis=1, tiled=True),
    )
    normed = layer_norm(hidden.astype(jnp.float32)).astype(jnp.bfloat16)
    query = jnp.dot(normed, full_query, preferred_element_type=jnp.float32).astype(jnp.bfloat16)
    key_proj = jnp.dot(normed, full_key, preferred_element_type=jnp.float32).astype(jnp.bfloat16)
    value_proj = jnp.dot(normed, full_value, preferred_element_type=jnp.float32).astype(
        jnp.bfloat16
    )
    shaped = query.reshape(parts, part_rows, groups, group_width).transpose(2, 0, 1, 3)
    query_pieces = shaped.reshape(shards, part_rows, group_width)
    kv_local = jnp.concatenate(
        [
            key_proj.reshape(local_rows, groups, group_width),
            value_proj.reshape(local_rows, groups, group_width),
        ],
        axis=2,
    )
    copies = jnp.broadcast_to(
        kv_local.transpose(1, 0, 2)[:, None], (groups, parts, local_rows, 2 * group_width)
    )
    copies = copies.reshape(shards, local_rows, 2 * group_width)
    query_got, kv_got = (
        lax.all_to_all(query_pieces, "seq", split_axis=0, concat_axis=0, tiled=True),
        lax.all_to_all(copies, "seq", split_axis=0, concat_axis=0, tiled=True),
    )
    key_value = kv_got.reshape(total_rows, 2 * group_width)
    count = shards * part_rows
    my_part = my_index % parts
    row_ids = jnp.arange(count, dtype=jnp.int32)
    query_pos = row_ids // part_rows * local_rows + my_part * part_rows + row_ids % part_rows
    queries = query_got.reshape(count, group_heads, head_size)
    key_rows = key_value[:, :group_width].reshape(total_rows, group_heads, head_size)
    value_rows = key_value[:, group_width:].reshape(total_rows, group_heads, head_size)
    seg_all = segment_ids(jnp.arange(total_rows, dtype=jnp.int32), utt_lengths)
    seg_query = segment_ids(query_pos, utt_lengths)
    query_block = math.gcd(512, count)
    blocks = count // query_block

    def attend_block(operands):
        block_query, block_seg = operands
        scores = (
            jnp.einsum("qhd,khd->hqk", block_query, key_rows, preferred_element_type=jnp.float32)
            * scale
        )
        allowed = (block_seg[:, None] == seg_all[None, :])[None]
        scores = jnp.where(allowed, scores, -1e30)
        peak = jnp.max(scores, axis=2, keepdims=True)
        expw = jnp.where(allowed, jnp.exp(scores - peak), 0.0)
        total_weight = jnp.sum(expw, axis=2)
        mixed = jnp.einsum(
            "hqk,khd->hqd",
            expw.astype(jnp.bfloat16),
            value_rows,
            preferred_element_type=jnp.float32,
        )
        mixed = mixed / total_weight[:, :, None]
        return mixed.transpose(1, 0, 2).astype(jnp.bfloat16)

    attended = lax.map(
        attend_block,
        (
            queries.reshape(blocks, query_block, group_heads, head_size),
            seg_query.reshape(blocks, query_block),
        ),
    )
    outgoing = attended.reshape(shards, part_rows, group_width)
    returned = lax.all_to_all(outgoing, "seq", split_axis=0, concat_axis=0, tiled=True)
    attended_local = (
        returned.reshape(groups, parts, part_rows, group_width)
        .transpose(1, 2, 0, 3)
        .reshape(local_rows, width)
    )
    return attended_local, full_output, full_conv_in, full_conv_out


def body(frames, lengths, w_query, w_key, w_value, w_output, conv_in, conv_taps, conv_out):
    hidden = frames[0]
    utt_lengths = lengths[0]
    shards = lax.axis_size("seq")
    my_index = lax.axis_index("seq")
    local_rows = hidden.shape[0]
    width = hidden.shape[1]
    total_rows = local_rows * shards
    if shards % 2 == 0 and width // shards == 128 and local_rows % 32 == 0:
        segments = segment_ids(jnp.arange(total_rows, dtype=jnp.int32), utt_lengths)
        attended_local, full_output, full_conv_in, full_conv_out = attention_call(
            shards,
            hidden,
            segments,
            w_query[0],
            w_key[0],
            w_value[0],
            (w_output[0], conv_in[0], conv_out[0]),
        )
    else:
        attended_local, full_output, full_conv_in, full_conv_out = attention_general(
            hidden,
            utt_lengths,
            w_query[0],
            w_key[0],
            w_value[0],
            w_output[0],
            conv_in[0],
            conv_out[0],
        )
    after_attn = hidden.astype(jnp.float32) + jnp.dot(
        attended_local, full_output, preferred_element_type=jnp.float32
    )
    conv_normed = layer_norm(after_attn).astype(jnp.bfloat16)
    gates = jnp.dot(conv_normed, full_conv_in, preferred_element_type=jnp.float32)
    glu = (gates[:, :width] * jax.nn.sigmoid(gates[:, width:])).astype(jnp.bfloat16)
    reach = KERNEL // 2
    padded = padded_2(glu, (("seq", 0),), KERNEL // 2)
    padded_pos = my_index * local_rows - reach + jnp.arange(local_rows + 2 * reach, dtype=jnp.int32)
    inside = (padded_pos >= 0) & (padded_pos < total_rows)
    padded_seg = jnp.where(inside, segment_ids(padded_pos, utt_lengths), -1)
    own_seg = padded_seg[reach : reach + local_rows]
    taps = conv_taps[0]
    depthwise = jnp.zeros((local_rows, width), jnp.float32)
    for offset in range(KERNEL):
        keep = padded_seg[offset : offset + local_rows] == own_seg
        term = padded[offset : offset + local_rows].astype(jnp.float32) * taps[offset].astype(
            jnp.float32
        )
        depthwise = depthwise + jnp.where(keep[:, None], term, 0.0)
    conv_act = layer_norm(depthwise)
    conv_act = (conv_act * jax.nn.sigmoid(conv_act)).astype(jnp.bfloat16)
    block_out = (
        after_attn + jnp.dot(conv_act, full_conv_out, preferred_element_type=jnp.float32)
    ).astype(jnp.bfloat16)
    passed = passed_along(block_out, "phase", 1)
    return passed[None]


def solution(mesh):
    in_specs = (
        P("phase", "seq", None),
        P("phase", None),
        P("phase", None, "seq"),
        P("phase", None, "seq"),
        P("phase", None, "seq"),
        P("phase", None, "seq"),
        P("phase", None, "seq"),
        P("phase", None, None),
        P("phase", None, "seq"),
    )
    out_specs = P("phase", "seq", None)
    return jax.shard_map(body, mesh=mesh, in_specs=in_specs, out_specs=out_specs, check_vma=False)
```

```python
import functools
import math

import jax
import jax.numpy as jnp
from jax import lax
from jax.experimental import pallas as pl
from jax.experimental.pallas import tpu as pltpu
from jax.sharding import PartitionSpec as P

HEADS = 16
KERNEL = 31
MESH = pl.DeviceIdType.MESH


def padded_2(block, sides, width):
    for axis, dim in sides:
        count = lax.axis_size(axis)
        forward = [(i, i + 1) for i in range(count - 1)]
        backward = [(target, source) for source, target in forward]
        low = lax.ppermute(
            lax.slice_in_dim(block, block.shape[dim] - width, None, axis=dim), axis, forward
        )
        high = lax.ppermute(lax.slice_in_dim(block, 0, width, axis=dim), axis, backward)
        block = jnp.concatenate([low, block, high], axis=dim)
    return block


def passed_along(block, axis, distance):
    devices = range(lax.axis_size(axis))
    route = [((i - distance) % len(devices), i) for i in devices]
    return lax.ppermute(block, axis, route)


def layer_norm(values):
    centre = values - jnp.mean(values, axis=-1, keepdims=True)
    spread = jnp.mean(centre * centre, axis=-1, keepdims=True)
    return centre * lax.rsqrt(spread + 1e-05)


def segment_ids(positions, lengths):
    order = jnp.arange(lengths.shape[0], dtype=jnp.int32)
    bounds = jnp.sum(jnp.where(order[None, :] <= order[:, None], lengths[None, :], 0), axis=1)
    return jnp.sum((positions[:, None] >= bounds[None, :]).astype(jnp.int32), axis=1)


def ring_index(place, shards):
    place = lax.rem(place + shards, shards)
    late = lax.div(place, shards // 2)
    return (1 - late) * (2 * place) + late * (2 * (shards - 1 - place) + 1)


def block_kernel(
    shards,
    head_size,
    frames_ref,
    seg_row_ref,
    seg_col_ref,
    near_ref,
    taps_ref,
    query_ref,
    key_ref,
    value_ref,
    w_a_ref,
    w_b_ref,
    w_c_ref,
    handed_ref,
    hidden,
    qkv,
    full_a_ref,
    full_b_ref,
    full_c_ref,
    attended_ref,
    after,
    gates,
    edge,
    padded,
    depthwise,
    leaving,
    normed,
    query,
    keys,
    values,
    outbox,
    send_sem,
    recv_sem,
    own_sem,
    out_send,
    out_recv,
    in_sem,
    edge_send,
    edge_recv,
    leave_send,
    leave_recv,
):
    rows = frames_ref.shape[0]
    depth = frames_ref.shape[1]
    width = query_ref.shape[1]
    loads_in = [pltpu.make_async_copy(frames_ref, hidden, in_sem.at[3])]
    for i, ref in enumerate((query_ref, key_ref, value_ref)):
        loads_in.append(
            pltpu.make_async_copy(ref, qkv.at[:, pl.ds(i * width, width)], in_sem.at[i])
        )
    for copy in loads_in:
        copy.start()
    steps = shards // 2
    me = lax.axis_index("seq")
    odd = lax.rem(me, 2)
    place = (1 - odd) * lax.div(me, 2) + odd * (shards - 1 - lax.div(me, 2))
    right, left = ring_index(place + 1, shards), ring_index(place - 1, shards)

    barrier = pltpu.get_barrier_semaphore()
    for away in range(1, shards):
        peer = lax.rem(me + away, shards)
        pl.semaphore_signal(barrier, inc=1, device_id={"seq": peer}, device_id_type=MESH)
    phase = lax.axis_index("phase")
    phases = lax.axis_size("phase")
    phase_next = lax.rem(phase + 1, phases)
    phase_back = lax.rem(phase + phases - 1, phases)
    for peer in (phase_next, phase_back):
        pl.semaphore_signal(barrier, inc=1, device_id={"phase": peer}, device_id_type=MESH)

    loads_in[0].wait()
    own_rows = pl.ds(pl.multiple_of(me * rows, rows), rows)
    normed[own_rows, :] = layer_norm(hidden[...].astype(jnp.float32)).astype(jnp.bfloat16)
    pl.semaphore_wait(barrier, shards + 1)

    pairs = ((w_a_ref, full_a_ref), (w_b_ref, full_b_ref), (w_c_ref, full_c_ref))

    def view(load, owner, half):
        if load == 0:
            first, size = (0, rows) if half is None else (half * (rows // 2), rows // 2)
            return normed.at[pl.ds(pl.multiple_of(owner * rows + first, 16), size), :]
        own, full = pairs[load - 1]
        depth, part = own.shape
        first, size = (0, depth) if half is None else (half * (depth // 2), depth // 2)
        return full.at[pl.ds(first, size), pl.ds(pl.multiple_of(owner * part, 128), part)]

    def hop(load, step, way):
        half = way if step == steps - 1 else None
        owner = ring_index(place - step if way == 0 else place + step, shards)
        target = view(load, owner, half)
        source = target
        if load > 0 and step == 0:
            source = pairs[load - 1][0]
            if half is not None:
                depth = source.shape[0] // 2
                source = source.at[pl.ds(half * depth, depth), :]
        return pltpu.make_async_remote_copy(
            src_ref=source,
            dst_ref=target,
            send_sem=send_sem.at[load, step, way],
            recv_sem=recv_sem.at[load, step, way],
            device_id={"seq": right if way == 0 else left},
            device_id_type=MESH,
        )

    def arrive(load, step):
        for way in range(2):
            hop(load, step, way).wait_recv()

    def send(load, step):
        for way in range(2):
            hop(load, step, way).start()

    def project(owner):
        at = pl.ds(pl.multiple_of(owner * rows, rows), rows)
        block = normed[at, :]
        both = jnp.dot(block, qkv[...], preferred_element_type=jnp.float32).astype(jnp.bfloat16)
        query[at, :] = both[:, :width] * jnp.bfloat16(1.0 / math.sqrt(head_size))
        keys[at, :] = both[:, width : 2 * width]
        values[at, :] = both[:, 2 * width :]

    kept = []
    send(0, 0)
    for load in (1, 2, 3):
        own, full = pairs[load - 1]
        part = own.shape[1]
        copy = pltpu.make_async_copy(
            own, full.at[:, pl.ds(pl.multiple_of(me * part, 128), part)], own_sem.at[load - 1]
        )
        copy.start()
        kept.append(copy)
    for copy in loads_in[1:]:
        copy.wait()
    project(me)
    for step in range(steps):
        arrive(0, step)
        if step < steps - 1:
            send(0, step + 1)
        if step == steps - 2:
            send(1, 0)
            send(2, 0)
        project(ring_index(place - 1 - step, shards))
        if step < steps - 1:
            project(ring_index(place + 1 + step, shards))

    lane = lax.broadcasted_iota(jnp.int32, (rows, width), 1)
    my_columns = pl.ds(pl.multiple_of(me * width, 128), width)

    def attend(owner):
        at = pl.ds(pl.multiple_of(owner * rows, rows), rows)
        block = query[at, :]
        allowed = seg_row_ref[at, :] == seg_col_ref[...]
        result = jnp.zeros((rows, width), jnp.float32)
        for head in range(width // head_size):
            mine = (lane >= head * head_size) & (lane < (head + 1) * head_size)
            scores = lax.dot_general(
                jnp.where(mine, block, jnp.bfloat16(0)),
                keys[...],
                (((1,), (1,)), ((), ())),
                preferred_element_type=jnp.float32,
            )
            scores = jnp.where(allowed, scores, -1e30)
            peak = jnp.max(scores, axis=1, keepdims=True)
            expw = jnp.exp(scores - peak)
            total = jnp.sum(expw, axis=1, keepdims=True)
            mixed = jnp.dot(
                expw.astype(jnp.bfloat16), values[...], preferred_element_type=jnp.float32
            )
            result = jnp.where(mine, mixed / total, result)
        return result.astype(jnp.bfloat16)

    def out_copy(away):
        peer = lax.rem(me + away, shards)
        return pltpu.make_async_remote_copy(
            src_ref=outbox.at[away - 1],
            dst_ref=attended_ref.at[:, my_columns],
            send_sem=out_send.at[away - 1],
            recv_sem=out_recv.at[away - 1],
            device_id={"seq": peer},
            device_id_type=MESH,
        )

    def forward(load, step):
        arrive(load, step)
        if step < steps - 1:
            send(load, step + 1)

    first = [(load, step) for step in range(steps) for load in (1, 2)]
    moved = 0
    for away in range(1, shards + 1):
        if away < shards:
            outbox[away - 1] = attend(lax.rem(me + away, shards))
            out_copy(away).start()
        else:
            attended_ref[:, my_columns] = attend(me)
        if away * 4 % shards == 0 and away < shards and moved < 3:
            forward(*first[moved])
            moved += 1
    send_last = False
    for load, step in first[moved:-1]:
        if load == 2 and step >= steps - 2:
            continue
        forward(load, step)
        if step >= steps - 2 and not send_last:
            send(3, 0)
            send_last = True
    for away in range(1, shards):
        out_copy(away).wait_recv()
    for copy in kept:
        copy.wait()
    tile = 2 * width
    for at in range(0, depth, tile):
        cols = slice(at, at + tile)
        after[:, cols] = hidden[:, cols].astype(jnp.float32) + jnp.dot(
            attended_ref[...], full_a_ref[:, cols], preferred_element_type=jnp.float32
        )
    conv_normed = layer_norm(after[...]).astype(jnp.bfloat16)
    part = w_b_ref.shape[1]

    def gate(owner):
        at = pl.ds(pl.multiple_of(owner * part, 128), part)
        gates[:, at] = jnp.dot(
            conv_normed, full_b_ref[:, at], preferred_element_type=jnp.float32
        )

    def gate_step(step):
        gate(ring_index(place - 1 - step, shards))
        if step < steps - 1:
            gate(ring_index(place + 1 + step, shards))

    gate(me)
    for step in range(steps - 2):
        gate_step(step)
    forward(2, steps - 2)
    gate_step(steps - 2)
    forward(3, 0)
    forward(2, steps - 1)
    gate_step(steps - 1)
    glu = (gates[:, :depth] * jax.nn.sigmoid(gates[:, depth:])).astype(jnp.bfloat16)
    margin = edge.shape[1]
    edge[0] = glu[:margin]
    edge[1] = glu[rows - margin :]

    def edge_copy(side):
        peer = lax.rem(me + (shards - 1 if side == 0 else 1), shards)
        return pltpu.make_async_remote_copy(
            src_ref=edge.at[side],
            dst_ref=edge.at[2 + side],
            send_sem=edge_send.at[side],
            recv_sem=edge_recv.at[side],
            device_id={"seq": peer},
            device_id_type=MESH,
        )

    edge_copy(0).start()
    edge_copy(1).start()
    padded[margin : margin + rows, :] = glu.astype(jnp.float32)
    edge_copy(0).wait_recv()
    edge_copy(1).wait_recv()
    padded[:margin, :] = edge[3].astype(jnp.float32)
    padded[margin + rows :, :] = edge[2].astype(jnp.float32)
    moved_last = 1
    reach = KERNEL // 2

    def taps_of(at):
        own = near_ref[margin : margin + rows, :]
        summed = jnp.zeros((rows, 128), jnp.float32)
        for offset in range(KERNEL):
            start = margin - reach + offset
            term = padded[start : start + rows, at : at + 128] * taps_ref[offset : offset + 1, at : at + 128]
            keep = near_ref[start : start + rows, :] == own
            summed = summed + jnp.where(keep, term, 0.0)
        depthwise[:, at : at + 128] = summed

    for at in range(0, depth, 128):
        taps_of(at)
        if at + 128 == depth // 2 and moved_last < steps - 1:
            forward(3, moved_last)
            moved_last += 1
    conv_act = layer_norm(depthwise[...])
    conv_act = (conv_act * jax.nn.sigmoid(conv_act)).astype(jnp.bfloat16)
    for step in range(moved_last, steps):
        forward(3, step)

    def leave(piece):
        cols = pl.ds(piece * tile, tile)
        return pltpu.make_async_remote_copy(
            src_ref=leaving.at[:, cols],
            dst_ref=handed_ref.at[:, cols],
            send_sem=leave_send.at[piece],
            recv_sem=leave_recv.at[piece],
            device_id={"phase": phase_next},
            device_id_type=MESH,
        )

    for piece in range(depth // tile):
        cols = slice(piece * tile, (piece + 1) * tile)
        leaving[:, cols] = (
            after[:, cols]
            + jnp.dot(conv_act, full_c_ref[:, cols], preferred_element_type=jnp.float32)
        ).astype(jnp.bfloat16)
        leave(piece).start()
    for away in range(1, shards):
        out_copy(away).wait_send()
    edge_copy(0).wait_send()
    edge_copy(1).wait_send()
    for load in range(4):
        for step in range(steps):
            for way in range(2):
                hop(load, step, way).wait_send()
    for piece in range(depth // tile):
        leave(piece).wait()


def block_call(shards, hidden, segments, near, taps, weights):
    rows, depth = hidden.shape
    width = weights[0].shape[1]
    total = rows * shards
    steps = shards // 2
    margin = (near.shape[0] - rows) // 2
    vmem = pl.BlockSpec(memory_space=pltpu.VMEM)
    anywhere = pl.BlockSpec(memory_space=pl.ANY)
    dma = pltpu.SemaphoreType.DMA
    bf16, f32 = jnp.bfloat16, jnp.float32
    return pl.pallas_call(
        functools.partial(block_kernel, shards, depth // HEADS),
        out_shape=jax.ShapeDtypeStruct((rows, depth), bf16),
        in_specs=[anywhere] + [vmem] * 4 + [anywhere] * 6,
        out_specs=vmem,
        scratch_shapes=[
            pltpu.VMEM((rows, depth), bf16),
            pltpu.VMEM((depth, 3 * width), bf16),
        ]
        + [pltpu.VMEM((w.shape[0], w.shape[1] * shards), bf16) for w in weights[3:]]
        + [
            pltpu.VMEM((rows, depth), bf16),
            pltpu.VMEM((rows, depth), f32),
            pltpu.VMEM((rows, 2 * depth), f32),
            pltpu.VMEM((4, margin, depth), bf16),
            pltpu.VMEM((rows + 2 * margin, depth), f32),
            pltpu.VMEM((rows, depth), f32),
            pltpu.VMEM((rows, depth), bf16),
            pltpu.VMEM((total, depth), bf16),
            pltpu.VMEM((total, width), bf16),
            pltpu.VMEM((total, width), bf16),
            pltpu.VMEM((total, width), bf16),
            pltpu.VMEM((shards - 1, rows, width), bf16),
            dma((4, steps, 2)),
            dma((4, steps, 2)),
            dma((3,)),
            dma((shards - 1,)),
            dma((shards - 1,)),
            dma((4,)),
            dma((2,)),
            dma((2,)),
            dma((depth // (2 * width),)),
            dma((depth // (2 * width),)),
        ],
        compiler_params=pltpu.CompilerParams(
            collective_id=0, has_side_effects=True, vmem_limit_bytes=56 * 1024 * 1024
        ),
    )(hidden, segments[:, None], segments[None, :], near, taps, *weights)


def attention_general(hidden, utt_lengths, w_query, w_key, w_value, w_output, conv_in, conv_out):
    shards = lax.axis_size("seq")
    my_index = lax.axis_index("seq")
    local_rows = hidden.shape[0]
    width = hidden.shape[1]
    total_rows = local_rows * shards
    head_size = width // HEADS
    scale = 1.0 / math.sqrt(head_size)
    groups = min(HEADS, shards)
    group_heads = HEADS // groups
    parts = shards // groups
    part_rows = local_rows // parts
    group_width = group_heads * head_size
    full_query, full_key, full_value, full_output, full_conv_in, full_conv_out = (
        lax.all_gather(w_query, "seq", axis=1, tiled=True),
        lax.all_gather(w_key, "seq", axis=1, tiled=True),
        lax.all_gather(w_value, "seq", axis=1, tiled=True),
        lax.all_gather(w_output, "seq", axis=1, tiled=True),
        lax.all_gather(conv_in, "seq", axis=1, tiled=True),
        lax.all_gather(conv_out, "seq", axis=1, tiled=True),
    )
    normed = layer_norm(hidden.astype(jnp.float32)).astype(jnp.bfloat16)
    query = jnp.dot(normed, full_query, preferred_element_type=jnp.float32).astype(jnp.bfloat16)
    key_proj = jnp.dot(normed, full_key, preferred_element_type=jnp.float32).astype(jnp.bfloat16)
    value_proj = jnp.dot(normed, full_value, preferred_element_type=jnp.float32).astype(
        jnp.bfloat16
    )
    shaped = query.reshape(parts, part_rows, groups, group_width).transpose(2, 0, 1, 3)
    query_pieces = shaped.reshape(shards, part_rows, group_width)
    kv_local = jnp.concatenate(
        [
            key_proj.reshape(local_rows, groups, group_width),
            value_proj.reshape(local_rows, groups, group_width),
        ],
        axis=2,
    )
    copies = jnp.broadcast_to(
        kv_local.transpose(1, 0, 2)[:, None], (groups, parts, local_rows, 2 * group_width)
    )
    copies = copies.reshape(shards, local_rows, 2 * group_width)
    query_got, kv_got = (
        lax.all_to_all(query_pieces, "seq", split_axis=0, concat_axis=0, tiled=True),
        lax.all_to_all(copies, "seq", split_axis=0, concat_axis=0, tiled=True),
    )
    key_value = kv_got.reshape(total_rows, 2 * group_width)
    count = shards * part_rows
    my_part = my_index % parts
    row_ids = jnp.arange(count, dtype=jnp.int32)
    query_pos = row_ids // part_rows * local_rows + my_part * part_rows + row_ids % part_rows
    queries = query_got.reshape(count, group_heads, head_size)
    key_rows = key_value[:, :group_width].reshape(total_rows, group_heads, head_size)
    value_rows = key_value[:, group_width:].reshape(total_rows, group_heads, head_size)
    seg_all = segment_ids(jnp.arange(total_rows, dtype=jnp.int32), utt_lengths)
    seg_query = segment_ids(query_pos, utt_lengths)
    query_block = math.gcd(512, count)
    blocks = count // query_block

    def attend_block(operands):
        block_query, block_seg = operands
        scores = (
            jnp.einsum("qhd,khd->hqk", block_query, key_rows, preferred_element_type=jnp.float32)
            * scale
        )
        allowed = (block_seg[:, None] == seg_all[None, :])[None]
        scores = jnp.where(allowed, scores, -1e30)
        peak = jnp.max(scores, axis=2, keepdims=True)
        expw = jnp.where(allowed, jnp.exp(scores - peak), 0.0)
        total_weight = jnp.sum(expw, axis=2)
        mixed = jnp.einsum(
            "hqk,khd->hqd",
            expw.astype(jnp.bfloat16),
            value_rows,
            preferred_element_type=jnp.float32,
        )
        mixed = mixed / total_weight[:, :, None]
        return mixed.transpose(1, 0, 2).astype(jnp.bfloat16)

    attended = lax.map(
        attend_block,
        (
            queries.reshape(blocks, query_block, group_heads, head_size),
            seg_query.reshape(blocks, query_block),
        ),
    )
    outgoing = attended.reshape(shards, part_rows, group_width)
    returned = lax.all_to_all(outgoing, "seq", split_axis=0, concat_axis=0, tiled=True)
    attended_local = (
        returned.reshape(groups, parts, part_rows, group_width)
        .transpose(1, 2, 0, 3)
        .reshape(local_rows, width)
    )
    return attended_local, full_output, full_conv_in, full_conv_out


def body(frames, lengths, w_query, w_key, w_value, w_output, conv_in, conv_taps, conv_out):
    hidden = frames[0]
    utt_lengths = lengths[0]
    shards = lax.axis_size("seq")
    my_index = lax.axis_index("seq")
    local_rows = hidden.shape[0]
    width = hidden.shape[1]
    total_rows = local_rows * shards
    phases = lax.axis_size("phase")
    if phases > 2 and shards % 8 == 0 and width // shards == 128 and local_rows % 32 == 0:
        segments = segment_ids(jnp.arange(total_rows, dtype=jnp.int32), utt_lengths)
        margin = 16
        near_pos = my_index * local_rows - margin
        near_pos = near_pos + jnp.arange(local_rows + 2 * margin, dtype=jnp.int32)
        inside = (near_pos >= 0) & (near_pos < total_rows)
        near = jnp.where(inside, segment_ids(near_pos, utt_lengths), -1)
        handed = block_call(
            shards,
            hidden,
            segments,
            jnp.broadcast_to(near[:, None], (near.shape[0], 128)),
            conv_taps[0].astype(jnp.float32),
            (w_query[0], w_key[0], w_value[0], w_output[0], conv_in[0], conv_out[0]),
        )
        return handed[None]
    attended_local, full_output, full_conv_in, full_conv_out = attention_general(
        hidden, utt_lengths, w_query[0], w_key[0], w_value[0], w_output[0], conv_in[0], conv_out[0]
    )
    after_attn = hidden.astype(jnp.float32) + jnp.dot(
        attended_local, full_output, preferred_element_type=jnp.float32
    )
    conv_normed = layer_norm(after_attn).astype(jnp.bfloat16)
    gates = jnp.dot(conv_normed, full_conv_in, preferred_element_type=jnp.float32)
    glu = (gates[:, :width] * jax.nn.sigmoid(gates[:, width:])).astype(jnp.bfloat16)
    reach = KERNEL // 2
    padded = padded_2(glu, (("seq", 0),), KERNEL // 2)
    padded_pos = my_index * local_rows - reach + jnp.arange(local_rows + 2 * reach, dtype=jnp.int32)
    inside = (padded_pos >= 0) & (padded_pos < total_rows)
    padded_seg = jnp.where(inside, segment_ids(padded_pos, utt_lengths), -1)
    own_seg = padded_seg[reach : reach + local_rows]
    taps = conv_taps[0]
    depthwise = jnp.zeros((local_rows, width), jnp.float32)
    for offset in range(KERNEL):
        keep = padded_seg[offset : offset + local_rows] == own_seg
        term = padded[offset : offset + local_rows].astype(jnp.float32) * taps[offset].astype(
            jnp.float32
        )
        depthwise = depthwise + jnp.where(keep[:, None], term, 0.0)
    conv_act = layer_norm(depthwise)
    conv_act = (conv_act * jax.nn.sigmoid(conv_act)).astype(jnp.bfloat16)
    block_out = (
        after_attn + jnp.dot(conv_act, full_conv_out, preferred_element_type=jnp.float32)
    ).astype(jnp.bfloat16)
    passed = passed_along(block_out, "phase", 1)
    return passed[None]


def solution(mesh):
    in_specs = (
        P("phase", "seq", None),
        P("phase", None),
        P("phase", None, "seq"),
        P("phase", None, "seq"),
        P("phase", None, "seq"),
        P("phase", None, "seq"),
        P("phase", None, "seq"),
        P("phase", None, None),
        P("phase", None, "seq"),
    )
    out_specs = P("phase", "seq", None)
    return jax.shard_map(body, mesh=mesh, in_specs=in_specs, out_specs=out_specs, check_vma=False)
```

```python
import functools
import math

import jax
import jax.numpy as jnp
from jax import lax
from jax.experimental import pallas as pl
from jax.experimental.pallas import tpu as pltpu
from jax.sharding import PartitionSpec as P

HEADS = 16
KERNEL = 31
MESH = pl.DeviceIdType.MESH


def padded_2(block, sides, width):
    for axis, dim in sides:
        count = lax.axis_size(axis)
        forward = [(i, i + 1) for i in range(count - 1)]
        backward = [(target, source) for source, target in forward]
        low = lax.ppermute(
            lax.slice_in_dim(block, block.shape[dim] - width, None, axis=dim), axis, forward
        )
        high = lax.ppermute(lax.slice_in_dim(block, 0, width, axis=dim), axis, backward)
        block = jnp.concatenate([low, block, high], axis=dim)
    return block


def passed_along(block, axis, distance):
    devices = range(lax.axis_size(axis))
    route = [((i - distance) % len(devices), i) for i in devices]
    return lax.ppermute(block, axis, route)


def layer_norm(values):
    centre = values - jnp.mean(values, axis=-1, keepdims=True)
    spread = jnp.mean(centre * centre, axis=-1, keepdims=True)
    return centre * lax.rsqrt(spread + 1e-05)


def segment_ids(positions, lengths):
    order = jnp.arange(lengths.shape[0], dtype=jnp.int32)
    bounds = jnp.sum(jnp.where(order[None, :] <= order[:, None], lengths[None, :], 0), axis=1)
    return jnp.sum((positions[:, None] >= bounds[None, :]).astype(jnp.int32), axis=1)


def ring_index(place, shards):
    place = lax.rem(place + shards, shards)
    late = lax.div(place, shards // 2)
    return (1 - late) * (2 * place) + late * (2 * (shards - 1 - place) + 1)


def block_kernel(
    shards,
    head_size,
    frames_ref,
    seg_row_ref,
    seg_col_ref,
    near_ref,
    taps_ref,
    query_ref,
    key_ref,
    value_ref,
    w_a_ref,
    w_b_ref,
    w_c_ref,
    handed_ref,
    hidden,
    qkv,
    full_a_ref,
    full_b_ref,
    full_c_ref,
    attended_ref,
    after,
    gates,
    edge,
    padded,
    depthwise,
    leaving,
    normed,
    query,
    keys,
    values,
    outbox,
    send_sem,
    recv_sem,
    own_sem,
    out_send,
    out_recv,
    in_sem,
    edge_send,
    edge_recv,
    leave_send,
    leave_recv,
):
    rows = frames_ref.shape[0]
    depth = frames_ref.shape[1]
    width = query_ref.shape[1]
    loads_in = [pltpu.make_async_copy(frames_ref, hidden, in_sem.at[3])]
    for i, ref in enumerate((query_ref, key_ref, value_ref)):
        loads_in.append(
            pltpu.make_async_copy(ref, qkv.at[:, pl.ds(i * width, width)], in_sem.at[i])
        )
    for copy in loads_in:
        copy.start()
    steps = shards // 2
    me = lax.axis_index("seq")
    odd = lax.rem(me, 2)
    place = (1 - odd) * lax.div(me, 2) + odd * (shards - 1 - lax.div(me, 2))
    right, left = ring_index(place + 1, shards), ring_index(place - 1, shards)

    barrier = pltpu.get_barrier_semaphore()
    for away in range(1, shards):
        peer = lax.rem(me + away, shards)
        pl.semaphore_signal(barrier, inc=1, device_id={"seq": peer}, device_id_type=MESH)
    phase = lax.axis_index("phase")
    phases = lax.axis_size("phase")
    phase_next = lax.rem(phase + 1, phases)
    phase_back = lax.rem(phase + phases - 1, phases)
    for peer in (phase_next, phase_back):
        pl.semaphore_signal(barrier, inc=1, device_id={"phase": peer}, device_id_type=MESH)

    loads_in[0].wait()
    own_rows = pl.ds(pl.multiple_of(me * rows, rows), rows)
    normed[own_rows, :] = layer_norm(hidden[...].astype(jnp.float32)).astype(jnp.bfloat16)
    pl.semaphore_wait(barrier, shards + 1)

    pairs = ((w_a_ref, full_a_ref), (w_b_ref, full_b_ref), (w_c_ref, full_c_ref))

    def view(load, owner, half):
        if load == 0:
            first, size = (0, rows) if half is None else (half * (rows // 2), rows // 2)
            return normed.at[pl.ds(pl.multiple_of(owner * rows + first, 16), size), :]
        own, full = pairs[load - 1]
        depth = own.shape[0]
        first, size = (0, depth) if half is None else (half * (depth // 2), depth // 2)
        return full.at[owner, pl.ds(first, size), :]

    def hop(load, step, way):
        half = way if step == steps - 1 else None
        owner = ring_index(place - step if way == 0 else place + step, shards)
        target = view(load, owner, half)
        source = target
        if load > 0 and step == 0:
            source = pairs[load - 1][0]
            if half is not None:
                depth = source.shape[0] // 2
                source = source.at[pl.ds(half * depth, depth), :]
        return pltpu.make_async_remote_copy(
            src_ref=source,
            dst_ref=target,
            send_sem=send_sem.at[load, step, way],
            recv_sem=recv_sem.at[load, step, way],
            device_id={"seq": right if way == 0 else left},
            device_id_type=MESH,
        )

    def arrive(load, step):
        for way in range(2):
            hop(load, step, way).wait_recv()

    def send(load, step):
        for way in range(2):
            hop(load, step, way).start()

    def project(owner):
        at = pl.ds(pl.multiple_of(owner * rows, rows), rows)
        block = normed[at, :]
        both = jnp.dot(block, qkv[...], preferred_element_type=jnp.float32).astype(jnp.bfloat16)
        query[at, :] = both[:, :width] * jnp.bfloat16(1.0 / math.sqrt(head_size))
        keys[at, :] = both[:, width : 2 * width]
        values[at, :] = both[:, 2 * width :]

    kept = []
    send(0, 0)
    for load in (1, 2, 3):
        own, full = pairs[load - 1]
        copy = pltpu.make_async_copy(own, full.at[me], own_sem.at[load - 1])
        copy.start()
        kept.append(copy)
    for copy in loads_in[1:]:
        copy.wait()
    project(me)
    for step in range(steps):
        arrive(0, step)
        if step < steps - 1:
            send(0, step + 1)
        if step == steps - 2:
            send(1, 0)
            send(2, 0)
        project(ring_index(place - 1 - step, shards))
        if step < steps - 1:
            project(ring_index(place + 1 + step, shards))

    lane = lax.broadcasted_iota(jnp.int32, (rows, width), 1)
    my_columns = pl.ds(pl.multiple_of(me * width, 128), width)

    def attend(owner):
        at = pl.ds(pl.multiple_of(owner * rows, rows), rows)
        block = query[at, :]
        allowed = seg_row_ref[at, :] == seg_col_ref[...]
        result = jnp.zeros((rows, width), jnp.float32)
        for head in range(width // head_size):
            mine = (lane >= head * head_size) & (lane < (head + 1) * head_size)
            scores = lax.dot_general(
                jnp.where(mine, block, jnp.bfloat16(0)),
                keys[...],
                (((1,), (1,)), ((), ())),
                preferred_element_type=jnp.float32,
            )
            scores = jnp.where(allowed, scores, -1e30)
            peak = jnp.max(scores, axis=1, keepdims=True)
            expw = jnp.exp(scores - peak)
            total = jnp.sum(expw, axis=1, keepdims=True)
            mixed = jnp.dot(
                expw.astype(jnp.bfloat16), values[...], preferred_element_type=jnp.float32
            )
            result = jnp.where(mine, mixed / total, result)
        return result.astype(jnp.bfloat16)

    def out_copy(away):
        peer = lax.rem(me + away, shards)
        return pltpu.make_async_remote_copy(
            src_ref=outbox.at[away - 1],
            dst_ref=attended_ref.at[:, my_columns],
            send_sem=out_send.at[away - 1],
            recv_sem=out_recv.at[away - 1],
            device_id={"seq": peer},
            device_id_type=MESH,
        )

    def forward(load, step):
        arrive(load, step)
        if step < steps - 1:
            send(load, step + 1)

    first = [(load, step) for step in range(steps) for load in (1, 2)]
    moved = 0
    for away in range(1, shards + 1):
        if away < shards:
            outbox[away - 1] = attend(lax.rem(me + away, shards))
            out_copy(away).start()
        else:
            attended_ref[:, my_columns] = attend(me)
        if away * 4 % shards == 0 and away < shards and moved < 3:
            forward(*first[moved])
            moved += 1
    send_last = False
    for load, step in first[moved:-1]:
        if load == 2 and step >= steps - 2:
            continue
        forward(load, step)
        if step >= steps - 2 and not send_last:
            send(3, 0)
            send_last = True
    for away in range(1, shards):
        out_copy(away).wait_recv()
    for copy in kept:
        copy.wait()
    tile = 2 * width

    def joined(full, pair):
        return jnp.concatenate([full[2 * pair], full[2 * pair + 1]], axis=1)

    for at in range(0, depth, tile):
        cols = slice(at, at + tile)
        after[:, cols] = hidden[:, cols].astype(jnp.float32) + jnp.dot(
            attended_ref[...], joined(full_a_ref, at // tile), preferred_element_type=jnp.float32
        )
    conv_normed = layer_norm(after[...]).astype(jnp.bfloat16)
    part = w_b_ref.shape[1]

    def gate(owner):
        at = pl.ds(pl.multiple_of(owner * part, 128), part)
        gates[:, at] = jnp.dot(
            conv_normed, full_b_ref[owner], preferred_element_type=jnp.float32
        )

    def gate_step(step):
        gate(ring_index(place - 1 - step, shards))
        if step < steps - 1:
            gate(ring_index(place + 1 + step, shards))

    gate(me)
    for step in range(steps - 2):
        gate_step(step)
    forward(2, steps - 2)
    gate_step(steps - 2)
    forward(3, 0)
    forward(2, steps - 1)
    gate_step(steps - 1)
    glu = (gates[:, :depth] * jax.nn.sigmoid(gates[:, depth:])).astype(jnp.bfloat16)
    margin = edge.shape[1]
    edge[0] = glu[:margin]
    edge[1] = glu[rows - margin :]

    def edge_copy(side):
        peer = lax.rem(me + (shards - 1 if side == 0 else 1), shards)
        return pltpu.make_async_remote_copy(
            src_ref=edge.at[side],
            dst_ref=edge.at[2 + side],
            send_sem=edge_send.at[side],
            recv_sem=edge_recv.at[side],
            device_id={"seq": peer},
            device_id_type=MESH,
        )

    edge_copy(0).start()
    edge_copy(1).start()
    padded[margin : margin + rows, :] = glu.astype(jnp.float32)
    edge_copy(0).wait_recv()
    edge_copy(1).wait_recv()
    padded[:margin, :] = edge[3].astype(jnp.float32)
    padded[margin + rows :, :] = edge[2].astype(jnp.float32)
    moved_last = 1
    reach = KERNEL // 2

    def taps_of(at):
        own = near_ref[margin : margin + rows, :]
        summed = jnp.zeros((rows, 128), jnp.float32)
        for offset in range(KERNEL):
            start = margin - reach + offset
            term = padded[start : start + rows, at : at + 128] * taps_ref[offset : offset + 1, at : at + 128]
            keep = near_ref[start : start + rows, :] == own
            summed = summed + jnp.where(keep, term, 0.0)
        depthwise[:, at : at + 128] = summed

    for at in range(0, depth, 128):
        taps_of(at)
        if at + 128 == depth // 2 and moved_last < steps - 1:
            forward(3, moved_last)
            moved_last += 1
    conv_act = layer_norm(depthwise[...])
    conv_act = (conv_act * jax.nn.sigmoid(conv_act)).astype(jnp.bfloat16)

    def leave(piece, owner):
        cols = pl.ds(pl.multiple_of(owner * width, 128), width)
        return pltpu.make_async_remote_copy(
            src_ref=leaving.at[:, cols],
            dst_ref=handed_ref.at[:, cols],
            send_sem=leave_send.at[piece],
            recv_sem=leave_recv.at[piece],
            device_id={"phase": phase_next},
            device_id_type=MESH,
        )

    sent = []

    def finish(owner):
        cols = pl.ds(pl.multiple_of(owner * width, 128), width)
        leaving[:, cols] = (
            after[:, cols]
            + jnp.dot(conv_act, full_c_ref[owner], preferred_element_type=jnp.float32)
        ).astype(jnp.bfloat16)
        copy = leave(len(sent), owner)
        copy.start()
        sent.append(copy)

    finish(me)
    for step in range(steps):
        if step >= moved_last:
            forward(3, step)
        finish(ring_index(place - 1 - step, shards))
        if step < steps - 1:
            finish(ring_index(place + 1 + step, shards))
    for away in range(1, shards):
        out_copy(away).wait_send()
    edge_copy(0).wait_send()
    edge_copy(1).wait_send()
    for load in range(4):
        for step in range(steps):
            for way in range(2):
                hop(load, step, way).wait_send()
    for copy in sent:
        copy.wait()


def block_call(shards, hidden, segments, near, taps, weights):
    rows, depth = hidden.shape
    width = weights[0].shape[1]
    total = rows * shards
    steps = shards // 2
    margin = (near.shape[0] - rows) // 2
    vmem = pl.BlockSpec(memory_space=pltpu.VMEM)
    anywhere = pl.BlockSpec(memory_space=pl.ANY)
    dma = pltpu.SemaphoreType.DMA
    bf16, f32 = jnp.bfloat16, jnp.float32
    return pl.pallas_call(
        functools.partial(block_kernel, shards, depth // HEADS),
        out_shape=jax.ShapeDtypeStruct((rows, depth), bf16),
        in_specs=[anywhere] + [vmem] * 4 + [anywhere] * 6,
        out_specs=vmem,
        scratch_shapes=[
            pltpu.VMEM((rows, depth), bf16),
            pltpu.VMEM((depth, 3 * width), bf16),
        ]
        + [pltpu.VMEM((shards, *w.shape), bf16) for w in weights[3:]]
        + [
            pltpu.VMEM((rows, depth), bf16),
            pltpu.VMEM((rows, depth), f32),
            pltpu.VMEM((rows, 2 * depth), f32),
            pltpu.VMEM((4, margin, depth), bf16),
            pltpu.VMEM((rows + 2 * margin, depth), f32),
            pltpu.VMEM((rows, depth), f32),
            pltpu.VMEM((rows, depth), bf16),
            pltpu.VMEM((total, depth), bf16),
            pltpu.VMEM((total, width), bf16),
            pltpu.VMEM((total, width), bf16),
            pltpu.VMEM((total, width), bf16),
            pltpu.VMEM((shards - 1, rows, width), bf16),
            dma((4, steps, 2)),
            dma((4, steps, 2)),
            dma((3,)),
            dma((shards - 1,)),
            dma((shards - 1,)),
            dma((4,)),
            dma((2,)),
            dma((2,)),
            dma((shards,)),
            dma((shards,)),
        ],
        compiler_params=pltpu.CompilerParams(
            collective_id=0, has_side_effects=True, vmem_limit_bytes=56 * 1024 * 1024
        ),
    )(hidden, segments[:, None], segments[None, :], near, taps, *weights)


def attention_general(hidden, utt_lengths, w_query, w_key, w_value, w_output, conv_in, conv_out):
    shards = lax.axis_size("seq")
    my_index = lax.axis_index("seq")
    local_rows = hidden.shape[0]
    width = hidden.shape[1]
    total_rows = local_rows * shards
    head_size = width // HEADS
    scale = 1.0 / math.sqrt(head_size)
    groups = min(HEADS, shards)
    group_heads = HEADS // groups
    parts = shards // groups
    part_rows = local_rows // parts
    group_width = group_heads * head_size
    full_query, full_key, full_value, full_output, full_conv_in, full_conv_out = (
        lax.all_gather(w_query, "seq", axis=1, tiled=True),
        lax.all_gather(w_key, "seq", axis=1, tiled=True),
        lax.all_gather(w_value, "seq", axis=1, tiled=True),
        lax.all_gather(w_output, "seq", axis=1, tiled=True),
        lax.all_gather(conv_in, "seq", axis=1, tiled=True),
        lax.all_gather(conv_out, "seq", axis=1, tiled=True),
    )
    normed = layer_norm(hidden.astype(jnp.float32)).astype(jnp.bfloat16)
    query = jnp.dot(normed, full_query, preferred_element_type=jnp.float32).astype(jnp.bfloat16)
    key_proj = jnp.dot(normed, full_key, preferred_element_type=jnp.float32).astype(jnp.bfloat16)
    value_proj = jnp.dot(normed, full_value, preferred_element_type=jnp.float32).astype(
        jnp.bfloat16
    )
    shaped = query.reshape(parts, part_rows, groups, group_width).transpose(2, 0, 1, 3)
    query_pieces = shaped.reshape(shards, part_rows, group_width)
    kv_local = jnp.concatenate(
        [
            key_proj.reshape(local_rows, groups, group_width),
            value_proj.reshape(local_rows, groups, group_width),
        ],
        axis=2,
    )
    copies = jnp.broadcast_to(
        kv_local.transpose(1, 0, 2)[:, None], (groups, parts, local_rows, 2 * group_width)
    )
    copies = copies.reshape(shards, local_rows, 2 * group_width)
    query_got, kv_got = (
        lax.all_to_all(query_pieces, "seq", split_axis=0, concat_axis=0, tiled=True),
        lax.all_to_all(copies, "seq", split_axis=0, concat_axis=0, tiled=True),
    )
    key_value = kv_got.reshape(total_rows, 2 * group_width)
    count = shards * part_rows
    my_part = my_index % parts
    row_ids = jnp.arange(count, dtype=jnp.int32)
    query_pos = row_ids // part_rows * local_rows + my_part * part_rows + row_ids % part_rows
    queries = query_got.reshape(count, group_heads, head_size)
    key_rows = key_value[:, :group_width].reshape(total_rows, group_heads, head_size)
    value_rows = key_value[:, group_width:].reshape(total_rows, group_heads, head_size)
    seg_all = segment_ids(jnp.arange(total_rows, dtype=jnp.int32), utt_lengths)
    seg_query = segment_ids(query_pos, utt_lengths)
    query_block = math.gcd(512, count)
    blocks = count // query_block

    def attend_block(operands):
        block_query, block_seg = operands
        scores = (
            jnp.einsum("qhd,khd->hqk", block_query, key_rows, preferred_element_type=jnp.float32)
            * scale
        )
        allowed = (block_seg[:, None] == seg_all[None, :])[None]
        scores = jnp.where(allowed, scores, -1e30)
        peak = jnp.max(scores, axis=2, keepdims=True)
        expw = jnp.where(allowed, jnp.exp(scores - peak), 0.0)
        total_weight = jnp.sum(expw, axis=2)
        mixed = jnp.einsum(
            "hqk,khd->hqd",
            expw.astype(jnp.bfloat16),
            value_rows,
            preferred_element_type=jnp.float32,
        )
        mixed = mixed / total_weight[:, :, None]
        return mixed.transpose(1, 0, 2).astype(jnp.bfloat16)

    attended = lax.map(
        attend_block,
        (
            queries.reshape(blocks, query_block, group_heads, head_size),
            seg_query.reshape(blocks, query_block),
        ),
    )
    outgoing = attended.reshape(shards, part_rows, group_width)
    returned = lax.all_to_all(outgoing, "seq", split_axis=0, concat_axis=0, tiled=True)
    attended_local = (
        returned.reshape(groups, parts, part_rows, group_width)
        .transpose(1, 2, 0, 3)
        .reshape(local_rows, width)
    )
    return attended_local, full_output, full_conv_in, full_conv_out


def body(frames, lengths, w_query, w_key, w_value, w_output, conv_in, conv_taps, conv_out):
    hidden = frames[0]
    utt_lengths = lengths[0]
    shards = lax.axis_size("seq")
    my_index = lax.axis_index("seq")
    local_rows = hidden.shape[0]
    width = hidden.shape[1]
    total_rows = local_rows * shards
    phases = lax.axis_size("phase")
    if phases > 2 and shards % 8 == 0 and width // shards == 128 and local_rows % 32 == 0:
        segments = segment_ids(jnp.arange(total_rows, dtype=jnp.int32), utt_lengths)
        margin = 16
        near_pos = my_index * local_rows - margin
        near_pos = near_pos + jnp.arange(local_rows + 2 * margin, dtype=jnp.int32)
        inside = (near_pos >= 0) & (near_pos < total_rows)
        near = jnp.where(inside, segment_ids(near_pos, utt_lengths), -1)
        handed = block_call(
            shards,
            hidden,
            segments,
            jnp.broadcast_to(near[:, None], (near.shape[0], 128)),
            conv_taps[0].astype(jnp.float32),
            (w_query[0], w_key[0], w_value[0], w_output[0], conv_in[0], conv_out[0]),
        )
        return handed[None]
    attended_local, full_output, full_conv_in, full_conv_out = attention_general(
        hidden, utt_lengths, w_query[0], w_key[0], w_value[0], w_output[0], conv_in[0], conv_out[0]
    )
    after_attn = hidden.astype(jnp.float32) + jnp.dot(
        attended_local, full_output, preferred_element_type=jnp.float32
    )
    conv_normed = layer_norm(after_attn).astype(jnp.bfloat16)
    gates = jnp.dot(conv_normed, full_conv_in, preferred_element_type=jnp.float32)
    glu = (gates[:, :width] * jax.nn.sigmoid(gates[:, width:])).astype(jnp.bfloat16)
    reach = KERNEL // 2
    padded = padded_2(glu, (("seq", 0),), KERNEL // 2)
    padded_pos = my_index * local_rows - reach + jnp.arange(local_rows + 2 * reach, dtype=jnp.int32)
    inside = (padded_pos >= 0) & (padded_pos < total_rows)
    padded_seg = jnp.where(inside, segment_ids(padded_pos, utt_lengths), -1)
    own_seg = padded_seg[reach : reach + local_rows]
    taps = conv_taps[0]
    depthwise = jnp.zeros((local_rows, width), jnp.float32)
    for offset in range(KERNEL):
        keep = padded_seg[offset : offset + local_rows] == own_seg
        term = padded[offset : offset + local_rows].astype(jnp.float32) * taps[offset].astype(
            jnp.float32
        )
        depthwise = depthwise + jnp.where(keep[:, None], term, 0.0)
    conv_act = layer_norm(depthwise)
    conv_act = (conv_act * jax.nn.sigmoid(conv_act)).astype(jnp.bfloat16)
    block_out = (
        after_attn + jnp.dot(conv_act, full_conv_out, preferred_element_type=jnp.float32)
    ).astype(jnp.bfloat16)
    passed = passed_along(block_out, "phase", 1)
    return passed[None]


def solution(mesh):
    in_specs = (
        P("phase", "seq", None),
        P("phase", None),
        P("phase", None, "seq"),
        P("phase", None, "seq"),
        P("phase", None, "seq"),
        P("phase", None, "seq"),
        P("phase", None, "seq"),
        P("phase", None, None),
        P("phase", None, "seq"),
    )
    out_specs = P("phase", "seq", None)
    return jax.shard_map(body, mesh=mesh, in_specs=in_specs, out_specs=out_specs, check_vma=False)
```
